32 devices in a mesh: dp: 4 (over z), ctx: 8 (over y, x, core).
Axes of the slice: x: 2, y: 2, z: 4, core: 2. Of those that a mesh axis runs over, the one named last changes fastest.
Arguments:
- inputs: bfloat16 [4, 1024, 1408], P('dp', 'ctx'), may hold values from -8 to 8
- cotangent: bfloat16 [4, 1024, 1408], P('dp', 'ctx'), may hold values from -6 to 6
- keep_mask: int32 [4], P('dp'), may hold values 0 or 1
- ln_gain: float32 [1408], replicated, may hold values from 0.1 to 1.9
- ln_bias: float32 [1408], replicated, may hold values from -4 to 4
- w_qkv: bfloat16 [1408, 4224], replicated, may hold values from -2 to 2
- qv_bias: float32 [2, 1408], replicated, may hold values from -6 to 6
- w_proj: bfloat16 [1408, 1408], replicated, may hold values from -0.15625 to 0.15625
- proj_bias: float32 [1408], replicated, may hold values from -4 to 4
Outputs:
- block_out: bfloat16 [4, 1024, 1408], P('dp', 'ctx')
- grad_inputs: bfloat16 [4, 1024, 1408], P('dp', 'ctx')
- grad_w_qkv: float32 [1408, 3, 1408], P('dp', None, 'ctx')
- grad_w_proj: float32 [1408, 1408], P('ctx', 'dp')
- grad_ln_gain: float32 [1408], P(('dp', 'ctx'))
- grad_ln_bias: float32 [1408], P(('dp', 'ctx'))
- grad_qv_bias: float32 [2, 1408], P(None, ('dp', 'ctx'))
- grad_proj_bias: float32 [1408], P(('dp', 'ctx'))
The draws below stay inside these ranges and needn't reach their ends.
All inputs are finite; a program needn't handle non-finite values. No bound on the sum of `keep_mask` on one device may be relied on, other than what follows from the above.
Results may differ from the reference program's by a relative error of at most 0.018.
The reference program's roundings to bfloat16 on the way count: a program that leaves them out, or rounds other values in their place, can miss the bound.
Values may be sent and summed in bfloat16 or wider, within the bound.
A program may use at most 128 MiB of HBM per device.

```python
import math
import jax
import jax.numpy as jnp
from jax import lax

D = 1408
HEADS = 16
SEQ = 1024
BATCH = 4


def draw_inputs(key, part):
    noise_draw = jax.random.normal(jax.random.fold_in(key, 1), (BATCH, SEQ, D), jnp.float32)
    return jnp.clip(noise_draw, -6.0, 6.0).astype(jnp.bfloat16)


def draw_w_qkv(key, part):
    base_draw = jnp.clip(jax.random.normal(jax.random.fold_in(key, 4), (D, 3 * D), jnp.float32), -5.0, 5.0) * (1.6 / math.sqrt(D))
    return base_draw.astype(jnp.bfloat16)


def with_ends(entries, key, least, high):
    shape = entries.shape
    place = [jax.random.randint(jax.random.fold_in(key, axis), (), 0, shape[axis]) for axis in range(len(shape))]
    entries = entries.at[tuple(place)].set(least)
    longest = shape.index(max(shape))
    place[longest] = (place[longest] + 1) % shape[longest]
    return entries.at[tuple(place)].set(high)


def level_of(rng, shape, split, low, high):
    level, own = 1.0, jax.random.fold_in(rng, 6)
    for dim, shards_of in split:
        steps = jnp.exp(jax.random.uniform(jax.random.fold_in(own, dim), (shards_of,), jnp.float32, low / len(split), high / len(split)))
        level = level * jnp.repeat(steps, shape[dim] // shards_of).reshape([-1 if axis == dim else 1 for axis in range(len(shape))])
    return level


def scatter_about(own_key, dims, deviation, reach, shards=(), dtype=jnp.bfloat16):
    array = jax.random.normal(own_key, dims, jnp.float32) * deviation
    if len(shards) > 0:
        array = level_of(own_key, dims, shards, -0.22, 0.18) * array
    return jnp.clip(array, min=-reach, max=reach).astype(dtype)


def setup_inputs(seed: int = 0) -> dict:
    streams_of = jax.random.split(jax.random.key(seed), 10)
    return {
        "inputs": draw_inputs(jax.random.fold_in(streams_of[9], 71), 0),
        "cotangent": scatter_about(streams_of[1], (BATCH, SEQ, D), 1.0, 6.0, ((0, 4), (1, 8))),
        "keep_mask": with_ends((jax.random.randint(streams_of[2], (BATCH,), 0, 4) < 3).astype(jnp.int32), jax.random.fold_in(streams_of[2], 1), 0, 1),
        "ln_gain": jnp.clip(1.0 + 0.18 * jax.random.normal(streams_of[3], (D,), jnp.float32), 0.1, 1.9),
        "ln_bias": scatter_about(streams_of[4], (D,), 0.3, 4.0, (), jnp.float32),
        "w_qkv": draw_w_qkv(jax.random.fold_in(streams_of[9], 71), 0),
        "qv_bias": scatter_about(streams_of[6], (2, D), 0.7, 6.0, (), jnp.float32),
        "w_proj": scatter_about(streams_of[7], (D, D), D ** -0.5, 0.15625),
        "proj_bias": scatter_about(streams_of[8], (D,), 0.3, 4.0, (), jnp.float32),
    }


eps = 1e-06
keep_rate = 0.75

def normalize(values):
    average = lax.optimization_barrier(jnp.mean(values, axis=-1, keepdims=True))
    centred = values - average
    variance = lax.optimization_barrier(jnp.mean(centred * centred, axis=-1, keepdims=True))
    inv_scale = lax.rsqrt(variance + eps)
    return (centred * inv_scale, inv_scale)

def reference(inputs, cotangent, keep_mask, ln_gain, ln_bias, w_qkv, qv_bias, w_proj, proj_bias):
    head_width = D // HEADS
    score_scale = head_width ** (-0.5)
    grad_scale = 1.0 / (BATCH * SEQ) ** 0.5
    bias_full = jnp.concatenate([qv_bias[0], jnp.zeros((D,), jnp.float32), qv_bias[1]])

    def split_heads(matrix):
        return matrix.reshape(SEQ, HEADS, head_width).transpose(1, 0, 2)

    def join_heads(stacked):
        return stacked.transpose(1, 0, 2).reshape(SEQ, D)

    def softmax_rows(queries, all_keys):
        scores = jnp.dot(queries, all_keys.T, preferred_element_type=jnp.float32) * score_scale
        row_max = lax.optimization_barrier(jnp.max(scores, axis=1, keepdims=True))
        log_total = row_max + jnp.log(lax.optimization_barrier(jnp.sum(jnp.exp(scores - row_max), axis=1, keepdims=True)))
        return jnp.exp(scores - log_total)

    def head_forward(pieces):
        queries, all_keys, all_values = pieces
        weights = softmax_rows(queries, all_keys).astype(jnp.bfloat16)
        return jnp.dot(weights, all_values, preferred_element_type=jnp.float32).astype(jnp.bfloat16)

    def head_backward(pieces):
        queries, all_keys, all_values, output, grad_out = pieces
        prob_rows = softmax_rows(queries, all_keys)
        weights = prob_rows.astype(jnp.bfloat16)
        row_delta = lax.optimization_barrier(jnp.sum(grad_out.astype(jnp.float32) * output.astype(jnp.float32), axis=1, keepdims=True))
        grad_values = jnp.dot(weights.T, grad_out, preferred_element_type=jnp.float32).astype(jnp.bfloat16)
        grad_probs = jnp.dot(grad_out, all_values.T, preferred_element_type=jnp.float32)
        grad_scores = (prob_rows * (grad_probs - row_delta) * score_scale).astype(jnp.bfloat16)
        grad_queries = jnp.dot(grad_scores, all_keys, preferred_element_type=jnp.float32).astype(jnp.bfloat16)
        grad_keys = jnp.dot(grad_scores.T, queries, preferred_element_type=jnp.float32).astype(jnp.bfloat16)
        return (grad_queries, grad_keys, grad_values)

    def sample_pass(totals, sample_item):
        tokens, grad_in, keep_flag = sample_item
        normed, inv_scale = normalize(tokens.astype(jnp.float32))
        layer_in = (normed * ln_gain + ln_bias).astype(jnp.bfloat16)
        packed = (jnp.dot(layer_in, w_qkv, preferred_element_type=jnp.float32) + bias_full).astype(jnp.bfloat16)
        queries = split_heads(packed[:, :D])
        all_keys = split_heads(packed[:, D:2 * D])
        all_values = split_heads(packed[:, 2 * D:])
        output = lax.map(head_forward, (queries, all_keys, all_values))
        attended = join_heads(output)
        survive = keep_flag.astype(jnp.float32) / keep_rate
        branch = jnp.dot(attended, w_proj, preferred_element_type=jnp.float32) + proj_bias
        result = (tokens.astype(jnp.float32) + survive * branch).astype(jnp.bfloat16)
        grad_branch = (grad_in.astype(jnp.float32) * survive).astype(jnp.bfloat16)
        grad_attended = jnp.dot(grad_branch, w_proj.T, preferred_element_type=jnp.float32).astype(jnp.bfloat16)
        grad_queries, grad_keys, grad_values = lax.map(head_backward, (queries, all_keys, all_values, output, split_heads(grad_attended)))
        grad_packed = jnp.concatenate([join_heads(grad_queries), join_heads(grad_keys), join_heads(grad_values)], axis=1)
        grad_layer = jnp.dot(grad_packed, w_qkv.T, preferred_element_type=jnp.float32)
        grad_norm = grad_layer * ln_gain
        centre_term = lax.optimization_barrier(jnp.mean(grad_norm, axis=-1, keepdims=True))
        slope_term = lax.optimization_barrier(jnp.mean(grad_norm * normed, axis=-1, keepdims=True))
        grad_tokens = (grad_in.astype(jnp.float32) + inv_scale * (grad_norm - centre_term - normed * slope_term)).astype(jnp.bfloat16)
        col_sums = lax.optimization_barrier(jnp.sum(grad_packed.astype(jnp.float32), axis=0))
        grad_terms = (jnp.dot(layer_in.T, grad_packed, preferred_element_type=jnp.float32), jnp.dot(attended.T, grad_branch, preferred_element_type=jnp.float32), lax.optimization_barrier(jnp.sum(grad_layer * normed, axis=0)), lax.optimization_barrier(jnp.sum(grad_layer, axis=0)), jnp.stack([col_sums[:D], col_sums[2 * D:]]), lax.optimization_barrier(jnp.sum(grad_branch.astype(jnp.float32), axis=0)))
        totals = jax.tree.map(lambda first, second: first + second, totals, grad_terms)
        return (totals, (result, grad_tokens))
    start_totals = (jnp.zeros((D, 3 * D), jnp.float32), jnp.zeros((D, D), jnp.float32), jnp.zeros((D,), jnp.float32), jnp.zeros((D,), jnp.float32), jnp.zeros((2, D), jnp.float32), jnp.zeros((D,), jnp.float32))
    totals, outputs = lax.scan(sample_pass, start_totals, (inputs, cotangent, keep_mask))
    block_out, grad_inputs = outputs
    scaled = jax.tree.map(lambda first: first * grad_scale, totals)
    return (block_out, grad_inputs, scaled[0].reshape(D, 3, D), scaled[1], scaled[2], scaled[3], scaled[4], scaled[5])
```

```python
import functools
import math

import jax
import jax.numpy as jnp
from jax import lax
from jax.experimental import pallas as pl
from jax.experimental.pallas import tpu as pltpu
from jax.sharding import PartitionSpec as P

HEADS = 16
PAD = 96
eps = 1e-06
keep_rate = 0.75
MESH = pl.DeviceIdType.MESH
f32 = jnp.float32
bf16 = jnp.bfloat16


def nt(left, right):
    return lax.dot_general(left, right, (((1,), (1,)), ((), ())), preferred_element_type=f32)


def nn(left, right):
    return jnp.dot(left, right, preferred_element_type=f32)


def turned(block):
    wide = block.astype(f32)
    fill = jnp.zeros((128 - PAD, wide.shape[1]), f32)
    return jnp.transpose(jnp.concatenate([wide, fill], axis=0))


def normalize(values):
    average = jnp.mean(values, axis=-1, keepdims=True)
    centred = values - average
    variance = jnp.mean(centred * centred, axis=-1, keepdims=True)
    inv_scale = lax.rsqrt(variance + eps)
    return centred * inv_scale, inv_scale


def kernel(
    n, ndp, hh, hw, grad_scale,
    survive_ref, x_ref, cot_ref, gain_ref, bias_ref, bqkv_ref, pbias_ref,
    wt_hbm, wp_hbm, wqkv_hbm, wproj_hbm,
    out_ref, gin_ref, gqk_ref, gvp_ref, small_ref,
    wt, wp, wqkv, wproj, lin, gb, qkv, tok, probs, att, ga, gan, dkv, gt,
    att_in, gt_in, gp, glt, rs_send, rs_recv, vec, vec_in, sums, sums_in,
    load_sem, ag_send, ag_recv, att_send, att_recv, gt_send, gt_recv,
    rs_ssem, rs_rsem, vs, vr, ss, sr, own_sem,
):
    tokens, width = x_ref.shape
    length = tokens * n
    me = lax.axis_index("ctx")
    my_dp = lax.axis_index("dp")
    chips = n // 2
    chip = me // 2
    core = lax.rem(me, 2)
    partner = 2 * chip + 1 - core
    scale = hw ** (-0.5)
    rows = width // ndp
    qb = 256

    loads = []
    for i, (src, dst) in enumerate(((wt_hbm, wt), (wp_hbm, wp), (wproj_hbm, wproj), (wqkv_hbm, wqkv))):
        load = pltpu.make_async_copy(src, dst, load_sem.at[i])
        load.start()
        loads.append(load)

    barrier = pltpu.get_barrier_semaphore()
    for o in range(1, n):
        pl.semaphore_signal(barrier, inc=1, device_id=(my_dp, lax.rem(me + o, n)), device_id_type=MESH)
    for o in range(1, ndp):
        pl.semaphore_signal(barrier, inc=1, device_id=(lax.rem(my_dp + o, ndp), me), device_id_type=MESH)

    def cols(block):
        return pl.ds(pl.multiple_of(block * tokens, 128), tokens)

    def gather_copy(buf, which, slot, block, target):
        return pltpu.make_async_remote_copy(
            src_ref=buf.at[:, cols(block)], dst_ref=buf.at[:, cols(block)],
            send_sem=ag_send.at[which, slot], recv_sem=ag_recv.at[which, slot],
            device_id=(my_dp, target), device_id_type=MESH)

    def gather_start(buf, which):
        for o in range(1, chips):
            gather_copy(buf, which, o, me, 2 * lax.rem(chip + o, chips) + core).start()
        gather_copy(buf, which, 0, me, partner).start()

    def gather_finish(buf, which):
        for o in range(1, chips):
            source = lax.rem(chip - o + chips, chips)
            block = 2 * source + core
            gather_copy(buf, which, o, block, partner).wait_recv()
            gather_copy(buf, which, chips + o, block, partner).start()
        gather_copy(buf, which, 0, partner, partner).wait_recv()
        for o in range(1, chips):
            source = lax.rem(chip - o + chips, chips)
            gather_copy(buf, which, chips + o, 2 * source + 1 - core, partner).wait_recv()
        for o in range(chips):
            gather_copy(buf, which, o, me, partner).wait_send()
        for o in range(1, chips):
            gather_copy(buf, which, chips + o, me, partner).wait_send()

    survive = survive_ref[0, 0]
    normed, _ = normalize(x_ref[...].astype(f32))
    lin[:, cols(me)] = jnp.transpose(normed * gain_ref[...] + bias_ref[...]).astype(bf16)
    pl.semaphore_wait(barrier, n - 1 + ndp - 1)
    gather_start(lin, 0)
    branch_grad = (cot_ref[...].astype(f32) * survive).astype(bf16).astype(f32)
    gb[:, cols(me)] = jnp.transpose(branch_grad).astype(bf16)
    gather_start(gb, 1)
    proj_sum = jnp.sum(branch_grad, axis=0, keepdims=True)

    loads[0].wait()
    gather_finish(lin, 0)

    def project(i, carry):
        where = pl.ds(pl.multiple_of(i * qb, qb), qb)
        block = (nn(wt[...], lin[:, where]) + bqkv_ref[...]).astype(bf16)
        for p in range(3):
            for h in range(hh):
                r = (p * hh + h) * PAD
                piece = block[r:r + PAD]
                qkv[p, h, :, where] = piece
                tok[p, h, where, :] = turned(piece).astype(bf16)
        return carry

    lax.fori_loop(0, length // qb, project, 0)

    def forward(i, carry):
        h = lax.rem(i, hh)
        where = pl.ds(pl.multiple_of((i // hh) * qb, qb), qb)
        scores = nn(tok[1, h][:, :PAD], qkv[0, h, :, where]) * scale
        top = jnp.max(scores, axis=0, keepdims=True)
        grown = jnp.exp(scores - top)
        total = jnp.sum(grown, axis=0, keepdims=True)
        prob = grown * (1.0 / total)
        probs[h, :, where] = prob
        att[h, :, where] = nn(qkv[2, h], prob.astype(bf16)).astype(bf16)
        return carry

    lax.fori_loop(0, hh * (length // qb), forward, 0)

    def spread_copy(src, dst, o, ssem, rsem):
        target = lax.rem(me + o, n)
        lead = (slice(None),) * (len(src.shape) - 1)
        return pltpu.make_async_remote_copy(
            src_ref=src.at[lead + (cols(target),)], dst_ref=dst.at[me],
            send_sem=ssem.at[o], recv_sem=rsem.at[o],
            device_id=(my_dp, target), device_id_type=MESH)

    def spread_start(src, dst, ssem, rsem, slot):
        for o in range(1, n):
            spread_copy(src, dst, o, ssem, rsem).start()
        lead = (slice(None),) * (len(src.shape) - 1)
        own = pltpu.make_async_copy(src.at[lead + (cols(me),)], dst.at[me], own_sem.at[slot])
        own.start()
        return own

    def spread_finish(src, dst, ssem, rsem, own):
        own.wait()
        for o in range(1, n):
            spread_copy(src, dst, o, ssem, rsem).wait_send()
            source = lax.rem(me - o + n, n)
            lead = (slice(None),) * (len(src.shape) - 1)
            pltpu.make_async_remote_copy(
                src_ref=src.at[lead + (cols(source),)], dst_ref=dst.at[source],
                send_sem=ssem.at[o], recv_sem=rsem.at[o],
                device_id=(my_dp, source), device_id_type=MESH).wait_recv()

    att_own = spread_start(att, att_in, att_send, att_recv, 0)

    loads[1].wait()
    gather_finish(gb, 1)

    def project_back(i, carry):
        where = pl.ds(pl.multiple_of(i * qb, qb), qb)
        block = nn(wp[...], gb[:, where]).astype(bf16)
        for h in range(hh):
            piece = block[h * PAD:(h + 1) * PAD]
            ga[h, :, where] = piece
            gan[h, where, :] = turned(piece).astype(bf16)
        return carry

    lax.fori_loop(0, length // qb, project_back, 0)
    dkv[...] = jnp.zeros_like(dkv)

    def backward(i, carry):
        h = lax.rem(i, hh)
        where = pl.ds(pl.multiple_of((i // hh) * qb, qb), qb)
        prob = probs[h, :, where]
        grad = ga[h, :, where]
        delta = jnp.sum(grad.astype(f32) * att[h, :, where].astype(f32), axis=0, keepdims=True)
        grad_probs = nn(tok[2, h][:, :PAD], grad)
        grad_scores = (prob * (grad_probs - delta) * scale).astype(bf16)
        gt[0, h, :, where] = nn(qkv[1, h], grad_scores).astype(bf16)
        dkv[0, h] += nn(grad_scores, tok[0, h, where, :])
        dkv[1, h] += nn(prob.astype(bf16), gan[h, where, :])
        return carry

    lax.fori_loop(0, hh * (length // qb), backward, 0)
    for p in range(2):
        for h in range(hh):
            gt[1 + p, h] = jnp.transpose(dkv[p, h])[:PAD].astype(bf16)

    gt_own = spread_start(gt, gt_in, gt_send, gt_recv, 1)

    def rs_copy(part, o):
        target = lax.rem(my_dp + o, ndp)
        return pltpu.make_async_remote_copy(
            src_ref=rs_send.at[part, target], dst_ref=rs_recv.at[part, o],
            send_sem=rs_ssem.at[part, o], recv_sem=rs_rsem.at[part, o],
            device_id=(target, me), device_id_type=MESH)

    half = 2 * hh * PAD
    for part in range(2):
        for o in list(range(1, ndp)) + [0]:
            target = lax.rem(my_dp + o, ndp)
            where = pl.ds(pl.multiple_of(target * rows, 16), rows)
            if part == 0:
                block = jnp.concatenate([
                    nt(lin[where, :], gt[2].reshape(hh * PAD, length)),
                    nt(gb[where, :], att[...].reshape(hh * PAD, length))], axis=1)
            else:
                block = nt(lin[where, :], gt[0:2].reshape(half, length))
            rs_send[part, target] = (block * grad_scale).astype(bf16)
            if o:
                rs_copy(part, o).start()

    spread_finish(att, att_in, att_send, att_recv, att_own)
    attended = jnp.concatenate(
        [att_in[g, h].astype(f32)[:hw] for g in range(n) for h in range(hh)], axis=0)
    attended = jnp.transpose(attended).astype(bf16)
    loads[2].wait()
    branch = nn(attended, wproj[...]) + pbias_ref[...]
    out_ref[...] = (x_ref[...].astype(f32) + survive * branch).astype(bf16)

    spread_finish(gt, gt_in, gt_send, gt_recv, gt_own)
    for p in range(3):
        gp[p * width:(p + 1) * width, :] = jnp.concatenate(
            [gt_in[g, p, h].astype(f32)[:hw] for g in range(n) for h in range(hh)], axis=0).astype(bf16)
    loads[3].wait()

    def layer_rows(i, carry):
        where = pl.ds(pl.multiple_of(i * 128, 128), 128)
        glt[where, :] = nn(wqkv[where, :], gp[...])
        return carry

    lax.fori_loop(0, width // 128, layer_rows, 0)
    grad_layer = jnp.transpose(glt[...])
    normed, inv_scale = normalize(x_ref[...].astype(f32))
    ones = jnp.ones((8, tokens), bf16)
    terms = [
        jnp.sum(grad_layer * normed, axis=0, keepdims=True),
        jnp.sum(grad_layer, axis=0, keepdims=True),
        nt(ones, gp[0:width, :])[0:1],
        nt(ones, gp[2 * width:3 * width, :])[0:1],
        proj_sum,
        jnp.zeros((3, width), f32),
    ]
    terms = jnp.concatenate(terms, axis=0) * grad_scale
    for j in range(ndp):
        vec[j] = terms[:, j * rows:(j + 1) * rows]

    def vec_copy(o):
        target = lax.rem(my_dp + o, ndp)
        return pltpu.make_async_remote_copy(
            src_ref=vec.at[target], dst_ref=vec_in.at[o], send_sem=vs.at[o], recv_sem=vr.at[o],
            device_id=(target, me), device_id_type=MESH)

    for o in range(1, ndp):
        vec_copy(o).start()
    grad_norm = grad_layer * gain_ref[...]
    centre_term = jnp.mean(grad_norm, axis=-1, keepdims=True)
    slope_term = jnp.mean(grad_norm * normed, axis=-1, keepdims=True)
    gin_ref[...] = (
        cot_ref[...].astype(f32) + inv_scale * (grad_norm - centre_term - normed * slope_term)
    ).astype(bf16)

    total = vec[my_dp]
    for o in range(1, ndp):
        vec_copy(o).wait()
        total = total + vec_in[o]
    sums[...] = total

    def sum_copy(o):
        return pltpu.make_async_remote_copy(
            src_ref=sums, dst_ref=sums_in.at[o], send_sem=ss.at[o], recv_sem=sr.at[o],
            device_id=(my_dp, lax.rem(me + o, n)), device_id_type=MESH)

    for o in range(1, n):
        sum_copy(o).start()

    for part, dst in ((0, gvp_ref), (1, gqk_ref)):
        acc = rs_send[part, my_dp].astype(f32)
        for o in range(1, ndp):
            rs_copy(part, o).wait()
            acc = acc + rs_recv[part, o].astype(f32)
        dst[...] = acc

    for o in range(1, n):
        sum_copy(o).wait()
        total = total + sums_in[o]
    small_ref[...] = total


def local(inputs, cotangent, keep_mask, ln_gain, ln_bias, w_qkv, qv_bias, w_proj, proj_bias):
    samples, tokens, width = inputs.shape
    n = lax.axis_size("ctx")
    ndp = lax.axis_size("dp")
    hh = HEADS // n
    hw = width // HEADS
    length = tokens * n
    rows = width // ndp
    half = 2 * hh * PAD
    me = lax.axis_index("ctx")
    grad_scale = 1.0 / math.sqrt(samples * ndp * length)
    survive = (keep_mask.astype(f32) / keep_rate).reshape(1, 1)
    bias_full = jnp.concatenate([qv_bias[0], jnp.zeros_like(qv_bias[0]), qv_bias[1]])
    wt, bqkv, wp = [], [], []
    for p in range(3):
        for h in range(hh):
            start = p * width + (me * hh + h) * hw
            wt.append(jnp.pad(lax.dynamic_slice_in_dim(w_qkv, start, hw, 1).T, ((0, PAD - hw), (0, 0))))
            bqkv.append(jnp.pad(lax.dynamic_slice_in_dim(bias_full, start, hw), (0, PAD - hw)))
    for h in range(hh):
        piece = lax.dynamic_slice_in_dim(w_proj, (me * hh + h) * hw, hw, 0)
        wp.append(jnp.pad(piece, ((0, PAD - hw), (0, 0))))
    wt = jnp.concatenate(wt, axis=0)
    wp = jnp.concatenate(wp, axis=0)
    bqkv = jnp.concatenate(bqkv).reshape(3 * hh * PAD, 1)

    vmem = pl.BlockSpec(memory_space=pltpu.VMEM)
    hbm = pl.BlockSpec(memory_space=pl.ANY)
    dma = pltpu.SemaphoreType.DMA
    out, gin, gqk, gvp, small = pl.pallas_call(
        functools.partial(kernel, n, ndp, hh, hw, grad_scale),
        out_shape=(
            jax.ShapeDtypeStruct((tokens, width), bf16),
            jax.ShapeDtypeStruct((tokens, width), bf16),
            jax.ShapeDtypeStruct((rows, half), f32),
            jax.ShapeDtypeStruct((rows, half), f32),
            jax.ShapeDtypeStruct((8, rows), f32),
        ),
        in_specs=[pl.BlockSpec(memory_space=pltpu.SMEM)] + [vmem] * 6 + [hbm] * 4,
        out_specs=(vmem,) * 5,
        scratch_shapes=[
            pltpu.VMEM((3 * hh * PAD, width), bf16),
            pltpu.VMEM((hh * PAD, width), bf16),
            pltpu.VMEM((width, 3 * width), bf16),
            pltpu.VMEM((width, width), bf16),
            pltpu.VMEM((width, length), bf16),
            pltpu.VMEM((width, length), bf16),
            pltpu.VMEM((3, hh, PAD, length), bf16),
            pltpu.VMEM((3, hh, length, 128), bf16),
            pltpu.VMEM((hh, length, length), f32),
            pltpu.VMEM((hh, PAD, length), bf16),
            pltpu.VMEM((hh, PAD, length), bf16),
            pltpu.VMEM((hh, length, 128), bf16),
            pltpu.VMEM((2, hh, length, 128), f32),
            pltpu.VMEM((3, hh, PAD, length), bf16),
            pltpu.VMEM((n, hh, PAD, tokens), bf16),
            pltpu.VMEM((n, 3, hh, PAD, tokens), bf16),
            pltpu.VMEM((3 * width, tokens), bf16),
            pltpu.VMEM((width, tokens), f32),
            pltpu.VMEM((2, ndp, rows, half), bf16),
            pltpu.VMEM((2, ndp, rows, half), bf16),
            pltpu.VMEM((ndp, 8, rows), f32),
            pltpu.VMEM((ndp, 8, rows), f32),
            pltpu.VMEM((8, rows), f32),
            pltpu.VMEM((n, 8, rows), f32),
            dma((4,)), dma((2, n)), dma((2, n)), dma((n,)), dma((n,)), dma((n,)), dma((n,)),
            dma((2, ndp)), dma((2, ndp)), dma((ndp,)), dma((ndp,)), dma((n,)), dma((n,)), dma((2,)),
        ],
        compiler_params=pltpu.CompilerParams(
            collective_id=0, has_side_effects=True, vmem_limit_bytes=63 * 1024 * 1024),
    )(
        survive, inputs[0], cotangent[0], ln_gain[None], ln_bias[None], bqkv, proj_bias[None],
        wt, wp, w_qkv, w_proj,
    )
    def heads(block):
        return block.reshape(rows, hh, PAD)[:, :, :hw].reshape(rows, hh * hw)

    part = half // 2
    grad_w_qkv = jnp.stack(
        [heads(gqk[:, :part]), heads(gqk[:, part:]), heads(gvp[:, :part])], axis=1)
    grad_w_proj = heads(gvp[:, part:]).T
    own = rows // n
    mine = lax.dynamic_slice_in_dim(small, me * own, own, 1)
    return (
        out[None], gin[None], grad_w_qkv, grad_w_proj,
        mine[0], mine[1], mine[2:4], mine[4],
    )


def solution(mesh):
    placed = (P("dp", "ctx", None), P("dp", "ctx", None), P("dp"), P(), P(), P(), P(), P(), P())
    return jax.shard_map(
        local,
        mesh=mesh,
        in_specs=placed,
        out_specs=(
            P("dp", "ctx", None),
            P("dp", "ctx", None),
            P("dp", None, "ctx"),
            P("ctx", "dp"),
            P(("dp", "ctx")),
            P(("dp", "ctx")),
            P(None, ("dp", "ctx")),
            P(("dp", "ctx")),
        ),
        check_vma=False,
    )
```

```python
import functools
import math

import jax
import jax.numpy as jnp
from jax import lax
from jax.experimental import pallas as pl
from jax.experimental.pallas import tpu as pltpu
from jax.sharding import PartitionSpec as P

HEADS = 16
PAD = 96
eps = 1e-06
keep_rate = 0.75
MESH = pl.DeviceIdType.MESH
f32 = jnp.float32
bf16 = jnp.bfloat16


def nt(left, right):
    return lax.dot_general(left, right, (((1,), (1,)), ((), ())), preferred_element_type=f32)


def nn(left, right):
    return jnp.dot(left, right, preferred_element_type=f32)


def turned(block):
    wide = block.astype(f32)
    fill = jnp.zeros((128 - PAD, wide.shape[1]), f32)
    return jnp.transpose(jnp.concatenate([wide, fill], axis=0))


def normalize(values):
    average = jnp.mean(values, axis=-1, keepdims=True)
    centred = values - average
    variance = jnp.mean(centred * centred, axis=-1, keepdims=True)
    inv_scale = lax.rsqrt(variance + eps)
    return centred * inv_scale, inv_scale


def kernel(
    n, ndp, hh, hw, grad_scale,
    survive_ref, x_ref, cot_ref, gain_ref, bias_ref, qvb_ref, pbias_ref,
    wqkv_hbm, wproj_hbm,
    out_ref, gin_ref, gproj_ref, gqkv_ref, small_ref,
    wt, wp, bqkv_ref, wqkv, wproj, lin, gb, qkv, tok, probs, att, ga, gan, dkv, gt,
    att_in, gt_in, gp, glt, ps_send, ps_recv, rs_send, rs_recv, vec, vec_in, sums, sums_in,
    load_sem, ag_send, ag_recv, att_send, att_recv, gt_send, gt_recv,
    ps_ssem, ps_rsem, rs_ssem, rs_rsem, vs, vr, ss, sr, own_sem,
):
    tokens, width = x_ref.shape
    length = tokens * n
    me = lax.axis_index("ctx")
    my_dp = lax.axis_index("dp")
    chips = n // 2
    chip = me // 2
    core = lax.rem(me, 2)
    partner = 2 * chip + 1 - core
    scale = hw ** (-0.5)
    rows = width // ndp
    qb = 256

    loads = []
    for i, (src, dst) in enumerate(((wqkv_hbm, wqkv), (wproj_hbm, wproj))):
        load = pltpu.make_async_copy(src, dst, load_sem.at[i])
        load.start()
        loads.append(load)

    barrier = pltpu.get_barrier_semaphore()
    for o in range(1, n):
        pl.semaphore_signal(barrier, inc=1, device_id=(my_dp, lax.rem(me + o, n)), device_id_type=MESH)
    for o in range(1, ndp):
        pl.semaphore_signal(barrier, inc=1, device_id=(lax.rem(my_dp + o, ndp), me), device_id_type=MESH)

    def cols(block):
        return pl.ds(pl.multiple_of(block * tokens, 128), tokens)

    def gather_copy(buf, which, slot, block, target):
        return pltpu.make_async_remote_copy(
            src_ref=buf.at[:, cols(block)], dst_ref=buf.at[:, cols(block)],
            send_sem=ag_send.at[which, slot], recv_sem=ag_recv.at[which, slot],
            device_id=(my_dp, target), device_id_type=MESH)

    square = chips == 4
    if square:
        along_x = chip + 1 - 2 * lax.rem(chip, 2)
        along_y = lax.rem(chip + 2, 4)
        onward = along_x * (1 - core) + along_y * core
        inward = along_y * (1 - core) + along_x * core
        sources = [None, inward, onward, 3 - chip]
        targets = [None, inward, onward]
    else:
        sources = [None] + [lax.rem(chip - o + chips, chips) for o in range(1, chips)]
        targets = [None] + [lax.rem(chip + o, chips) for o in range(1, chips)]

    def gather_start(buf, which):
        for o in range(1, len(targets)):
            gather_copy(buf, which, o, me, 2 * targets[o] + core).start()
        gather_copy(buf, which, 0, me, partner).start()

    def gather_step(buf, which, o):
        block = 2 * sources[o] + core
        gather_copy(buf, which, o, block, partner).wait_recv()
        if square and o == 1:
            gather_copy(buf, which, 3, block, 2 * onward + core).start()
        gather_copy(buf, which, chips + o, block, partner).start()

    def gather_finish(buf, which):
        gather_copy(buf, which, 0, partner, partner).wait_recv()
        for o in range(1, chips):
            gather_copy(buf, which, chips + o, 2 * sources[o] + 1 - core, partner).wait_recv()
        for o in range(chips):
            gather_copy(buf, which, o, me, partner).wait_send()
        for o in range(1, chips):
            gather_copy(buf, which, chips + o, me, partner).wait_send()

    survive = survive_ref[0, 0]
    normed, _ = normalize(x_ref[...].astype(f32))
    lin[:, cols(me)] = jnp.transpose(normed * gain_ref[...] + bias_ref[...]).astype(bf16)
    pl.semaphore_wait(barrier, n - 1 + ndp - 1)
    gather_start(lin, 0)
    branch_grad = (cot_ref[...].astype(f32) * survive).astype(bf16).astype(f32)
    gb[:, cols(me)] = jnp.transpose(branch_grad).astype(bf16)
    proj_sum = jnp.sum(branch_grad, axis=0, keepdims=True)

    row_id = lax.broadcasted_iota(jnp.int32, (PAD, 256), 0)
    col_id = lax.broadcasted_iota(jnp.int32, (PAD, 256), 1)
    row_sq = lax.broadcasted_iota(jnp.int32, (PAD, PAD), 0)
    col_sq = lax.broadcasted_iota(jnp.int32, (PAD, PAD), 1)
    loads[0].wait()
    for h in range(hh):
        off = (me * hh + h) * hw
        begin = (off // 128) * 128
        begin = begin - 128 * (begin // (width - 128))
        pick = (col_id == row_id + (off - begin)) & (row_id < hw)
        ones_at = jnp.where(pick, 1.0, 0.0)
        for p in range(3):
            r = (p * hh + h) * PAD
            window = wqkv[:, pl.ds(pl.multiple_of(p * width + begin, 128), 256)]
            wt[r:r + PAD, :] = nt(ones_at.astype(bf16), window).astype(bf16)
            if p == 1:
                bqkv_ref[r:r + PAD, :] = jnp.zeros((PAD, 1), f32)
            else:
                entries = qvb_ref[p // 2:p // 2 + 1, pl.ds(pl.multiple_of(begin, 128), 256)]
                bqkv_ref[r:r + PAD, :] = jnp.sum(
                    jnp.where(pick, entries, 0.0), axis=1, keepdims=True)
    for o in range(1, len(targets)):
        gather_step(lin, 0, o)
    gather_start(gb, 1)
    for o in range(len(targets), chips):
        gather_step(lin, 0, o)
    loads[1].wait()
    for h in range(hh):
        off = (me * hh + h) * hw
        begin = (off // 16) * 16
        pick = (col_sq == row_sq + (off - begin)) & (row_sq < hw)
        window = wproj[pl.ds(pl.multiple_of(begin, 16), PAD), :]
        wp[h * PAD:(h + 1) * PAD, :] = nn(jnp.where(pick, 1.0, 0.0).astype(bf16), window).astype(bf16)
    gather_finish(lin, 0)

    def project(i, carry):
        where = pl.ds(pl.multiple_of(i * qb, qb), qb)
        block = (nn(wt[...], lin[:, where]) + bqkv_ref[...]).astype(bf16)
        for p in range(3):
            for h in range(hh):
                r = (p * hh + h) * PAD
                piece = block[r:r + PAD]
                qkv[p, h, :, where] = piece
                tok[p, h, where, :] = turned(piece).astype(bf16)
        return carry

    lax.fori_loop(0, length // qb, project, 0)
    gather_step(gb, 1, 1)

    def forward(i, carry):
        h = lax.rem(i, hh)
        where = pl.ds(pl.multiple_of((i // hh) * qb, qb), qb)
        scores = nn(tok[1, h][:, :PAD], qkv[0, h, :, where]) * scale
        top = jnp.max(scores, axis=0, keepdims=True)
        grown = jnp.exp(scores - top)
        total = jnp.sum(grown, axis=0, keepdims=True)
        prob = grown * (1.0 / total)
        probs[h, :, where] = prob
        att[h, :, where] = nn(qkv[2, h], prob.astype(bf16)).astype(bf16)
        return carry

    lax.fori_loop(0, hh * (length // qb), forward, 0)

    def spread_copy(src, dst, o, ssem, rsem, lanes, slot, target):
        lead = (slice(None),) * (len(src.shape) - 1)
        return pltpu.make_async_remote_copy(
            src_ref=src.at[lead + (cols(lanes),)], dst_ref=dst.at[slot],
            send_sem=ssem.at[o], recv_sem=rsem.at[o],
            device_id=(my_dp, target), device_id_type=MESH)

    def spread_start(src, dst, ssem, rsem, own_slot):
        for o in range(1, n):
            target = lax.rem(me + o, n)
            spread_copy(src, dst, o, ssem, rsem, target, me, target).start()
        lead = (slice(None),) * (len(src.shape) - 1)
        own = pltpu.make_async_copy(src.at[lead + (cols(me),)], dst.at[me], own_sem.at[own_slot])
        own.start()
        return own

    def spread_finish(src, dst, ssem, rsem, own):
        own.wait()
        for o in range(1, n):
            target = lax.rem(me + o, n)
            source = lax.rem(me - o + n, n)
            spread_copy(src, dst, o, ssem, rsem, target, me, target).wait_send()
            spread_copy(src, dst, o, ssem, rsem, source, source, source).wait_recv()

    for o in range(2, chips):
        gather_step(gb, 1, o)
    att_own = spread_start(att, att_in, att_send, att_recv, 0)

    gather_finish(gb, 1)

    def project_back(i, carry):
        where = pl.ds(pl.multiple_of(i * qb, qb), qb)
        block = nn(wp[...], gb[:, where]).astype(bf16)
        for h in range(hh):
            piece = block[h * PAD:(h + 1) * PAD]
            ga[h, :, where] = piece
            gan[h, where, :] = turned(piece).astype(bf16)
        return carry

    lax.fori_loop(0, length // qb, project_back, 0)
    def ps_copy(o):
        target = lax.rem(my_dp + o, ndp)
        return pltpu.make_async_remote_copy(
            src_ref=ps_send.at[target], dst_ref=ps_recv.at[o],
            send_sem=ps_ssem.at[o], recv_sem=ps_rsem.at[o],
            device_id=(target, me), device_id_type=MESH)

    def rs_copy(h, o):
        target = lax.rem(my_dp + o, ndp)
        return pltpu.make_async_remote_copy(
            src_ref=rs_send.at[h, target], dst_ref=rs_recv.at[h, o],
            send_sem=rs_ssem.at[h, o], recv_sem=rs_rsem.at[h, o],
            device_id=(target, me), device_id_type=MESH)

    order = list(range(1, ndp)) + [0]

    def compact(pieces, to):
        pieces = [piece.astype(f32)[:hw] for piece in pieces]
        more = to - hw * len(pieces)
        if more:
            pieces.append(jnp.zeros((more, length), f32))
        return jnp.concatenate(pieces, axis=0).astype(bf16)

    left = compact([att[h] for h in range(hh)], ps_send.shape[1])
    for o in order:
        target = lax.rem(my_dp + o, ndp)
        where = pl.ds(pl.multiple_of(target * rows, 16), rows)
        ps_send[target] = (nt(left, gb[where, :]) * grad_scale).astype(bf16)
        if o:
            ps_copy(o).start()

    dkv[...] = jnp.zeros_like(dkv)
    gt_owns = []
    for h in range(hh):
        def backward(i, carry, h=h):
            where = pl.ds(pl.multiple_of(i * qb, qb), qb)
            prob = probs[h, :, where]
            grad = ga[h, :, where]
            delta = jnp.sum(grad.astype(f32) * att[h, :, where].astype(f32), axis=0, keepdims=True)
            grad_probs = nn(tok[2, h][:, :PAD], grad)
            grad_scores = (prob * (grad_probs - delta) * scale).astype(bf16)
            gt[h, 0, :, where] = nn(qkv[1, h], grad_scores).astype(bf16)
            dkv[0, h] += nn(grad_scores, tok[0, h, where, :])
            dkv[1, h] += nn(prob.astype(bf16), gan[h, where, :])
            return carry

        lax.fori_loop(0, length // qb, backward, 0)
        for p in range(2):
            gt[h, 1 + p] = jnp.transpose(dkv[p, h])[:PAD].astype(bf16)
        gt_owns.append(spread_start(gt.at[h], gt_in.at[h], gt_send.at[h], gt_recv.at[h], 1 + h))
        left = compact([gt[h, p] for p in range(3)], rs_send.shape[2])
        for o in order:
            target = lax.rem(my_dp + o, ndp)
            where = pl.ds(pl.multiple_of(target * rows, 16), rows)
            rs_send[h, target] = (nt(left, lin[where, :]) * grad_scale).astype(bf16)
            if o:
                rs_copy(h, o).start()

    spread_finish(att, att_in, att_send, att_recv, att_own)
    attended = jnp.concatenate(
        [att_in[g, h].astype(f32)[:hw] for g in range(n) for h in range(hh)], axis=0)
    attended = jnp.transpose(attended).astype(bf16)
    branch = nn(attended, wproj[...]) + pbias_ref[...]
    out_ref[...] = (x_ref[...].astype(f32) + survive * branch).astype(bf16)

    for h in range(hh):
        spread_finish(gt.at[h], gt_in.at[h], gt_send.at[h], gt_recv.at[h], gt_owns[h])
    for p in range(3):
        gp[p * width:(p + 1) * width, :] = jnp.concatenate(
            [gt_in[h, g, p].astype(f32)[:hw] for g in range(n) for h in range(hh)], axis=0).astype(bf16)

    def layer_rows(i, carry):
        where = pl.ds(pl.multiple_of(i * 128, 128), 128)
        glt[where, :] = nn(wqkv[where, :], gp[...])
        return carry

    lax.fori_loop(0, width // 128, layer_rows, 0)
    grad_layer = jnp.transpose(glt[...])
    normed, inv_scale = normalize(x_ref[...].astype(f32))
    ones = jnp.ones((8, tokens), bf16)
    terms = [
        jnp.sum(grad_layer * normed, axis=0, keepdims=True),
        jnp.sum(grad_layer, axis=0, keepdims=True),
        nt(ones, gp[0:width, :])[0:1],
        nt(ones, gp[2 * width:3 * width, :])[0:1],
        proj_sum,
        jnp.zeros((3, width), f32),
    ]
    terms = jnp.concatenate(terms, axis=0) * grad_scale
    for j in range(ndp):
        vec[j] = terms[:, j * rows:(j + 1) * rows]

    def vec_copy(o):
        target = lax.rem(my_dp + o, ndp)
        return pltpu.make_async_remote_copy(
            src_ref=vec.at[target], dst_ref=vec_in.at[o], send_sem=vs.at[o], recv_sem=vr.at[o],
            device_id=(target, me), device_id_type=MESH)

    for o in range(1, ndp):
        vec_copy(o).start()
    grad_norm = grad_layer * gain_ref[...]
    centre_term = jnp.mean(grad_norm, axis=-1, keepdims=True)
    slope_term = jnp.mean(grad_norm * normed, axis=-1, keepdims=True)
    gin_ref[...] = (
        cot_ref[...].astype(f32) + inv_scale * (grad_norm - centre_term - normed * slope_term)
    ).astype(bf16)

    total = vec[my_dp]
    for o in range(1, ndp):
        vec_copy(o).wait()
        total = total + vec_in[o]
    sums[...] = total

    def sum_copy(o):
        return pltpu.make_async_remote_copy(
            src_ref=sums, dst_ref=sums_in.at[o], send_sem=ss.at[o], recv_sem=sr.at[o],
            device_id=(my_dp, lax.rem(me + o, n)), device_id_type=MESH)

    for o in range(1, n):
        sum_copy(o).start()

    acc = ps_send[my_dp].astype(f32)
    for o in range(1, ndp):
        ps_copy(o).wait()
        acc = acc + ps_recv[o].astype(f32)
    gproj_ref[...] = acc
    for h in range(hh):
        acc = rs_send[h, my_dp].astype(f32)
        for o in range(1, ndp):
            rs_copy(h, o).wait()
            acc = acc + rs_recv[h, o].astype(f32)
        gqkv_ref[h] = acc

    for o in range(1, n):
        sum_copy(o).wait()
        total = total + sums_in[o]
    small_ref[...] = total


def local(inputs, cotangent, keep_mask, ln_gain, ln_bias, w_qkv, qv_bias, w_proj, proj_bias):
    samples, tokens, width = inputs.shape
    n = lax.axis_size("ctx")
    ndp = lax.axis_size("dp")
    hh = HEADS // n
    hw = width // HEADS
    length = tokens * n
    rows = width // ndp
    across = -(-hh * hw // 16) * 16
    tall = -(-3 * hw // 16) * 16
    me = lax.axis_index("ctx")
    grad_scale = 1.0 / math.sqrt(samples * ndp * length)
    survive = (keep_mask.astype(f32) / keep_rate).reshape(1, 1)
    vmem = pl.BlockSpec(memory_space=pltpu.VMEM)
    hbm = pl.BlockSpec(memory_space=pl.ANY)
    dma = pltpu.SemaphoreType.DMA
    out, gin, gproj, gqkv, small = pl.pallas_call(
        functools.partial(kernel, n, ndp, hh, hw, grad_scale),
        out_shape=(
            jax.ShapeDtypeStruct((tokens, width), bf16),
            jax.ShapeDtypeStruct((tokens, width), bf16),
            jax.ShapeDtypeStruct((across, rows), f32),
            jax.ShapeDtypeStruct((hh, tall, rows), f32),
            jax.ShapeDtypeStruct((8, rows), f32),
        ),
        in_specs=[pl.BlockSpec(memory_space=pltpu.SMEM)] + [vmem] * 6 + [hbm] * 2,
        out_specs=(vmem,) * 5,
        scratch_shapes=[
            pltpu.VMEM((3 * hh * PAD, width), bf16),
            pltpu.VMEM((hh * PAD, width), bf16),
            pltpu.VMEM((3 * hh * PAD, 1), f32),
            pltpu.VMEM((width, 3 * width), bf16),
            pltpu.VMEM((width, width), bf16),
            pltpu.VMEM((width, length), bf16),
            pltpu.VMEM((width, length), bf16),
            pltpu.VMEM((3, hh, PAD, length), bf16),
            pltpu.VMEM((3, hh, length, 128), bf16),
            pltpu.VMEM((hh, length, length), f32),
            pltpu.VMEM((hh, PAD, length), bf16),
            pltpu.VMEM((hh, PAD, length), bf16),
            pltpu.VMEM((hh, length, 128), bf16),
            pltpu.VMEM((2, hh, length, 128), f32),
            pltpu.VMEM((hh, 3, PAD, length), bf16),
            pltpu.VMEM((n, hh, PAD, tokens), bf16),
            pltpu.VMEM((hh, n, 3, PAD, tokens), bf16),
            pltpu.VMEM((3 * width, tokens), bf16),
            pltpu.VMEM((width, tokens), f32),
            pltpu.VMEM((ndp, across, rows), bf16),
            pltpu.VMEM((ndp, across, rows), bf16),
            pltpu.VMEM((hh, ndp, tall, rows), bf16),
            pltpu.VMEM((hh, ndp, tall, rows), bf16),
            pltpu.VMEM((ndp, 8, rows), f32),
            pltpu.VMEM((ndp, 8, rows), f32),
            pltpu.VMEM((8, rows), f32),
            pltpu.VMEM((n, 8, rows), f32),
            dma((2,)), dma((2, n)), dma((2, n)), dma((n,)), dma((n,)), dma((hh, n)), dma((hh, n)),
            dma((ndp,)), dma((ndp,)), dma((hh, ndp)), dma((hh, ndp)),
            dma((ndp,)), dma((ndp,)), dma((n,)), dma((n,)), dma((1 + hh,)),
        ],
        compiler_params=pltpu.CompilerParams(
            collective_id=0, has_side_effects=True, vmem_limit_bytes=63 * 1024 * 1024),
    )(
        survive, inputs[0], cotangent[0], ln_gain[None], ln_bias[None], qv_bias, proj_bias[None],
        w_qkv, w_proj,
    )
    grad_w_qkv = gqkv[:, :3 * hw].reshape(hh, 3, hw, rows).transpose(3, 1, 0, 2).reshape(rows, 3, hh * hw)
    grad_w_proj = gproj[:hh * hw]
    own = rows // n
    mine = lax.dynamic_slice_in_dim(small, me * own, own, 1)
    return (
        out[None], gin[None], grad_w_qkv, grad_w_proj,
        mine[0], mine[1], mine[2:4], mine[4],
    )


def solution(mesh):
    placed = (P("dp", "ctx", None), P("dp", "ctx", None), P("dp"), P(), P(), P(), P(), P(), P())
    return jax.shard_map(
        local,
        mesh=mesh,
        in_specs=placed,
        out_specs=(
            P("dp", "ctx", None),
            P("dp", "ctx", None),
            P("dp", None, "ctx"),
            P("ctx", "dp"),
            P(("dp", "ctx")),
            P(("dp", "ctx")),
            P(None, ("dp", "ctx")),
            P(("dp", "ctx")),
        ),
        check_vma=False,
    )
```

```python
import functools
import math

import jax
import jax.numpy as jnp
from jax import lax
from jax.experimental import pallas as pl
from jax.experimental.pallas import tpu as pltpu
from jax.sharding import PartitionSpec as P

HEADS = 16
PAD = 96
eps = 1e-06
keep_rate = 0.75
MESH = pl.DeviceIdType.MESH
f32 = jnp.float32
bf16 = jnp.bfloat16


def nt(left, right):
    return lax.dot_general(left, right, (((1,), (1,)), ((), ())), preferred_element_type=f32)


def nn(left, right):
    return jnp.dot(left, right, preferred_element_type=f32)


def turned(block):
    wide = block.astype(f32)
    fill = jnp.zeros((128 - PAD, wide.shape[1]), f32)
    return jnp.transpose(jnp.concatenate([wide, fill], axis=0))


def normalize(values):
    average = jnp.mean(values, axis=-1, keepdims=True)
    centred = values - average
    variance = jnp.mean(centred * centred, axis=-1, keepdims=True)
    inv_scale = lax.rsqrt(variance + eps)
    return centred * inv_scale, inv_scale


def kernel(
    n, ndp, hh, hw, grad_scale,
    survive_ref, x_ref, cot_ref, gain_ref, bias_ref, qvb_ref, pbias_ref,
    wqkv_hbm, wproj_hbm,
    out_ref, gin_ref, gproj_ref, gqkv_ref, small_ref,
    wt, wp, bqkv_ref, wqkv, wproj, lin, gb, qkv, tok, probs, att, ga, gan, dkv, gt,
    att_in, gt_in, gp, glt, ps_send, ps_recv, rs_send, rs_recv, vec, vec_in, sums, sums_in,
    load_sem, ag_send, ag_recv, att_send, att_recv, gt_send, gt_recv,
    ps_ssem, ps_rsem, rs_ssem, rs_rsem, vs, vr, ss, sr, own_sem,
):
    tokens, width = x_ref.shape
    length = tokens * n
    me = lax.axis_index("ctx")
    my_dp = lax.axis_index("dp")
    chips = n // 2
    chip = me // 2
    core = lax.rem(me, 2)
    partner = 2 * chip + 1 - core
    scale = hw ** (-0.5)
    rows = width // ndp
    qb = 256

    loads = []
    for i, (src, dst) in enumerate(((wqkv_hbm, wqkv), (wproj_hbm, wproj))):
        load = pltpu.make_async_copy(src, dst, load_sem.at[i])
        load.start()
        loads.append(load)

    barrier = pltpu.get_barrier_semaphore()
    for o in range(1, n):
        pl.semaphore_signal(barrier, inc=1, device_id=(my_dp, lax.rem(me + o, n)), device_id_type=MESH)
    for o in range(1, ndp):
        pl.semaphore_signal(barrier, inc=1, device_id=(lax.rem(my_dp + o, ndp), me), device_id_type=MESH)

    def cols(block):
        return pl.ds(pl.multiple_of(block * tokens, 128), tokens)

    def gather_copy(buf, which, slot, block, target):
        return pltpu.make_async_remote_copy(
            src_ref=buf.at[:, cols(block)], dst_ref=buf.at[:, cols(block)],
            send_sem=ag_send.at[which, slot], recv_sem=ag_recv.at[which, slot],
            device_id=(my_dp, target), device_id_type=MESH)

    square = chips == 4
    if square:
        along_x = chip + 1 - 2 * lax.rem(chip, 2)
        along_y = lax.rem(chip + 2, 4)
        onward = along_x * (1 - core) + along_y * core
        inward = along_y * (1 - core) + along_x * core
        sources = [None, inward, onward, 3 - chip]
        targets = [None, inward, onward]
    else:
        sources = [None] + [lax.rem(chip - o + chips, chips) for o in range(1, chips)]
        targets = [None] + [lax.rem(chip + o, chips) for o in range(1, chips)]

    def gather_start(buf, which):
        for o in range(1, len(targets)):
            gather_copy(buf, which, o, me, 2 * targets[o] + core).start()
        gather_copy(buf, which, 0, me, partner).start()

    def gather_step(buf, which, o):
        block = 2 * sources[o] + core
        gather_copy(buf, which, o, block, partner).wait_recv()
        if square and o == 1:
            gather_copy(buf, which, 3, block, 2 * onward + core).start()
        gather_copy(buf, which, chips + o, block, partner).start()

    def gather_finish(buf, which):
        gather_copy(buf, which, 0, partner, partner).wait_recv()
        for o in range(1, chips):
            gather_copy(buf, which, chips + o, 2 * sources[o] + 1 - core, partner).wait_recv()
        for o in range(chips):
            gather_copy(buf, which, o, me, partner).wait_send()
        for o in range(1, chips):
            gather_copy(buf, which, chips + o, me, partner).wait_send()

    survive = survive_ref[0, 0]
    normed, _ = normalize(x_ref[...].astype(f32))
    lin[:, cols(me)] = jnp.transpose(normed * gain_ref[...].reshape(1, width) + bias_ref[...].reshape(1, width)).astype(bf16)
    pl.semaphore_wait(barrier, n - 1 + ndp - 1)
    gather_start(lin, 0)
    branch_grad = (cot_ref[...].astype(f32) * survive).astype(bf16).astype(f32)
    gb[:, cols(me)] = jnp.transpose(branch_grad).astype(bf16)
    proj_sum = jnp.sum(branch_grad, axis=0, keepdims=True)

    row_id = lax.broadcasted_iota(jnp.int32, (PAD, 256), 0)
    col_id = lax.broadcasted_iota(jnp.int32, (PAD, 256), 1)
    row_sq = lax.broadcasted_iota(jnp.int32, (PAD, PAD), 0)
    col_sq = lax.broadcasted_iota(jnp.int32, (PAD, PAD), 1)
    loads[0].wait()
    for h in range(hh):
        off = (me * hh + h) * hw
        begin = (off // 128) * 128
        begin = begin - 128 * (begin // (width - 128))
        pick = (col_id == row_id + (off - begin)) & (row_id < hw)
        ones_at = jnp.where(pick, 1.0, 0.0)
        for p in range(3):
            r = (p * hh + h) * PAD
            window = wqkv[:, pl.ds(pl.multiple_of(p * width + begin, 128), 256)]
            wt[r:r + PAD, :] = nt(ones_at.astype(bf16), window).astype(bf16)
            if p == 1:
                bqkv_ref[r:r + PAD, :] = jnp.zeros((PAD, 1), f32)
            else:
                entries = qvb_ref[p // 2:p // 2 + 1, pl.ds(pl.multiple_of(begin, 128), 256)]
                bqkv_ref[r:r + PAD, :] = jnp.sum(
                    jnp.where(pick, entries, 0.0), axis=1, keepdims=True)
    for o in range(1, len(targets)):
        gather_step(lin, 0, o)
    gather_start(gb, 1)
    for o in range(len(targets), chips):
        gather_step(lin, 0, o)
    loads[1].wait()
    for h in range(hh):
        off = (me * hh + h) * hw
        begin = (off // 16) * 16
        pick = (col_sq == row_sq + (off - begin)) & (row_sq < hw)
        window = wproj[pl.ds(pl.multiple_of(begin, 16), PAD), :]
        wp[h * PAD:(h + 1) * PAD, :] = nn(jnp.where(pick, 1.0, 0.0).astype(bf16), window).astype(bf16)
    gather_finish(lin, 0)

    def project(i, carry):
        where = pl.ds(pl.multiple_of(i * qb, qb), qb)
        block = (nn(wt[...], lin[:, where]) + bqkv_ref[...]).astype(bf16)
        for p in range(3):
            for h in range(hh):
                r = (p * hh + h) * PAD
                piece = block[r:r + PAD]
                qkv[p, h, :, where] = piece
                tok[p, h, where, :] = turned(piece).astype(bf16)
        return carry

    lax.fori_loop(0, length // qb, project, 0)
    gather_step(gb, 1, 1)

    def forward(i, carry):
        h = lax.rem(i, hh)
        where = pl.ds(pl.multiple_of((i // hh) * qb, qb), qb)
        scores = nn(tok[1, h][:, :PAD], qkv[0, h, :, where]) * scale
        top = jnp.max(scores, axis=0, keepdims=True)
        grown = jnp.exp(scores - top)
        total = jnp.sum(grown, axis=0, keepdims=True)
        prob = grown * (1.0 / total)
        probs[h, :, where] = prob
        att[h, :, where] = nn(qkv[2, h], prob.astype(bf16)).astype(bf16)
        return carry

    lax.fori_loop(0, hh * (length // qb), forward, 0)

    def spread_copy(src, dst, o, ssem, rsem, lanes, slot, target):
        lead = (slice(None),) * (len(src.shape) - 1)
        return pltpu.make_async_remote_copy(
            src_ref=src.at[lead + (cols(lanes),)], dst_ref=dst.at[slot],
            send_sem=ssem.at[o], recv_sem=rsem.at[o],
            device_id=(my_dp, target), device_id_type=MESH)

    def spread_start(src, dst, ssem, rsem, own_slot):
        for o in range(1, n):
            target = lax.rem(me + o, n)
            spread_copy(src, dst, o, ssem, rsem, target, me, target).start()
        lead = (slice(None),) * (len(src.shape) - 1)
        own = pltpu.make_async_copy(src.at[lead + (cols(me),)], dst.at[me], own_sem.at[own_slot])
        own.start()
        return own

    def spread_finish(src, dst, ssem, rsem, own):
        own.wait()
        for o in range(1, n):
            target = lax.rem(me + o, n)
            source = lax.rem(me - o + n, n)
            spread_copy(src, dst, o, ssem, rsem, target, me, target).wait_send()
            spread_copy(src, dst, o, ssem, rsem, source, source, source).wait_recv()

    for o in range(2, chips):
        gather_step(gb, 1, o)
    att_own = spread_start(att, att_in, att_send, att_recv, 0)

    gather_finish(gb, 1)

    def project_back(i, carry):
        where = pl.ds(pl.multiple_of(i * qb, qb), qb)
        block = nn(wp[...], gb[:, where]).astype(bf16)
        for h in range(hh):
            piece = block[h * PAD:(h + 1) * PAD]
            ga[h, :, where] = piece
            gan[h, where, :] = turned(piece).astype(bf16)
        return carry

    lax.fori_loop(0, length // qb, project_back, 0)
    parts = [(ps_send, ps_recv, ps_ssem, ps_rsem)] + [
        (rs_send.at[h], rs_recv.at[h], rs_ssem.at[h], rs_rsem.at[h]) for h in range(hh)]
    halving = ndp == 4
    parity = lax.rem(my_dp, 2)
    beside = my_dp + 1 - 2 * parity
    far = lax.rem(my_dp + 2, ndp)

    def reduce_copy(part, k):
        send, recv, ssem, rsem = parts[part]
        if not halving:
            block = target = lax.rem(my_dp + k, ndp)
        elif k < 2:
            block, target = 1 - parity + 2 * k, beside
        else:
            block = target = far
        return pltpu.make_async_remote_copy(
            src_ref=send.at[block], dst_ref=recv.at[k],
            send_sem=ssem.at[k], recv_sem=rsem.at[k],
            device_id=(target, me), device_id_type=MESH)

    def reduce_first(part, left, buf):
        if halving:
            order = [(1 - parity, 0), (3 - parity, 1), (parity, None), (parity + 2, None)]
        else:
            order = [(lax.rem(my_dp + o, ndp), o) for o in range(1, ndp)] + [(my_dp, None)]
        for block, k in order:
            where = pl.ds(pl.multiple_of(block * rows, 16), rows)
            parts[part][0][block] = (nt(left, buf[where, :]) * grad_scale).astype(bf16)
            if k is not None:
                reduce_copy(part, k).start()

    def reduce_second(part):
        if halving:
            send, recv, _, _ = parts[part]
            for k in range(2):
                reduce_copy(part, k).wait()
            send[far] = (send[far].astype(f32) + recv[far // 2].astype(f32)).astype(bf16)
            reduce_copy(part, 2).start()

    def reduce_last(part):
        send, recv, _, _ = parts[part]
        acc = send[my_dp].astype(f32)
        if halving:
            reduce_copy(part, 2).wait()
            return acc + recv[my_dp // 2].astype(f32) + recv[2].astype(f32)
        for o in range(1, ndp):
            reduce_copy(part, o).wait()
            acc = acc + recv[o].astype(f32)
        return acc

    def compact(pieces, to):
        pieces = [piece.astype(f32)[:hw] for piece in pieces]
        more = to - hw * len(pieces)
        if more:
            pieces.append(jnp.zeros((more, length), f32))
        return jnp.concatenate(pieces, axis=0).astype(bf16)

    left = compact([att[h] for h in range(hh)], ps_send.shape[1])
    reduce_first(0, left, gb)

    dkv[...] = jnp.zeros_like(dkv)
    gt_owns = []
    for h in range(hh):
        def backward(i, carry, h=h):
            where = pl.ds(pl.multiple_of(i * qb, qb), qb)
            prob = probs[h, :, where]
            grad = ga[h, :, where]
            delta = jnp.sum(grad.astype(f32) * att[h, :, where].astype(f32), axis=0, keepdims=True)
            grad_probs = nn(tok[2, h][:, :PAD], grad)
            grad_scores = (prob * (grad_probs - delta) * scale).astype(bf16)
            gt[h, 0, :, where] = nn(qkv[1, h], grad_scores).astype(bf16)
            dkv[0, h] += nn(grad_scores, tok[0, h, where, :])
            dkv[1, h] += nn(prob.astype(bf16), gan[h, where, :])
            return carry

        lax.fori_loop(0, length // qb, backward, 0)
        for p in range(2):
            gt[h, 1 + p] = jnp.transpose(dkv[p, h])[:PAD].astype(bf16)
        gt_owns.append(spread_start(gt.at[h], gt_in.at[h], gt_send.at[h], gt_recv.at[h], 1 + h))
        left = compact([gt[h, p] for p in range(3)], rs_send.shape[2])
        reduce_first(1 + h, left, lin)
        reduce_second(h)

    spread_finish(att, att_in, att_send, att_recv, att_own)
    attended = jnp.concatenate(
        [att_in[g, h].astype(f32)[:hw] for g in range(n) for h in range(hh)], axis=0)
    attended = jnp.transpose(attended).astype(bf16)
    branch = nn(attended, wproj[...]) + pbias_ref[...].reshape(1, width)
    out_ref[...] = (x_ref[...].astype(f32) + survive * branch).astype(bf16)

    for h in range(hh):
        spread_finish(gt.at[h], gt_in.at[h], gt_send.at[h], gt_recv.at[h], gt_owns[h])
    for p in range(3):
        gp[p * width:(p + 1) * width, :] = jnp.concatenate(
            [gt_in[h, g, p].astype(f32)[:hw] for g in range(n) for h in range(hh)], axis=0).astype(bf16)

    def layer_rows(i, carry):
        where = pl.ds(pl.multiple_of(i * 128, 128), 128)
        glt[where, :] = nn(wqkv[where, :], gp[...])
        return carry

    lax.fori_loop(0, width // 128, layer_rows, 0)
    reduce_second(hh)
    grad_layer = jnp.transpose(glt[...])
    normed, inv_scale = normalize(x_ref[...].astype(f32))
    ones = jnp.ones((8, tokens), bf16)
    terms = [
        jnp.sum(grad_layer * normed, axis=0, keepdims=True),
        jnp.sum(grad_layer, axis=0, keepdims=True),
        nt(ones, gp[0:width, :])[0:1],
        nt(ones, gp[2 * width:3 * width, :])[0:1],
        proj_sum,
        jnp.zeros((3, width), f32),
    ]
    terms = jnp.concatenate(terms, axis=0) * grad_scale
    for j in range(ndp):
        vec[j] = terms[:, j * rows:(j + 1) * rows]

    def vec_copy(o):
        target = lax.rem(my_dp + o, ndp)
        return pltpu.make_async_remote_copy(
            src_ref=vec.at[target], dst_ref=vec_in.at[o], send_sem=vs.at[o], recv_sem=vr.at[o],
            device_id=(target, me), device_id_type=MESH)

    for o in range(1, ndp):
        vec_copy(o).start()
    grad_norm = grad_layer * gain_ref[...].reshape(1, width)
    centre_term = jnp.mean(grad_norm, axis=-1, keepdims=True)
    slope_term = jnp.mean(grad_norm * normed, axis=-1, keepdims=True)
    gin_ref[...] = (
        cot_ref[...].astype(f32) + inv_scale * (grad_norm - centre_term - normed * slope_term)
    ).astype(bf16)

    total = vec[my_dp]
    for o in range(1, ndp):
        vec_copy(o).wait()
        total = total + vec_in[o]
    sums[...] = total

    def sum_copy(o):
        return pltpu.make_async_remote_copy(
            src_ref=sums, dst_ref=sums_in.at[o], send_sem=ss.at[o], recv_sem=sr.at[o],
            device_id=(my_dp, lax.rem(me + o, n)), device_id_type=MESH)

    for o in range(1, n):
        sum_copy(o).start()

    gproj_ref[...] = reduce_last(0)
    for h in range(hh):
        gqkv_ref[h] = reduce_last(1 + h)

    for o in range(1, n):
        sum_copy(o).wait()
        total = total + sums_in[o]
    small_ref[...] = total


def local(inputs, cotangent, keep_mask, ln_gain, ln_bias, w_qkv, qv_bias, w_proj, proj_bias):
    samples, tokens, width = inputs.shape
    n = lax.axis_size("ctx")
    ndp = lax.axis_size("dp")
    hh = HEADS // n
    hw = width // HEADS
    length = tokens * n
    rows = width // ndp
    across = -(-hh * hw // 16) * 16
    tall = -(-3 * hw // 16) * 16
    me = lax.axis_index("ctx")
    grad_scale = 1.0 / math.sqrt(samples * ndp * length)
    survive = (keep_mask.astype(f32) / keep_rate).reshape(1, 1)
    vmem = pl.BlockSpec(memory_space=pltpu.VMEM)
    hbm = pl.BlockSpec(memory_space=pl.ANY)
    dma = pltpu.SemaphoreType.DMA
    out, gin, gproj, gqkv, small = pl.pallas_call(
        functools.partial(kernel, n, ndp, hh, hw, grad_scale),
        out_shape=(
            jax.ShapeDtypeStruct((tokens, width), bf16),
            jax.ShapeDtypeStruct((tokens, width), bf16),
            jax.ShapeDtypeStruct((across, rows), f32),
            jax.ShapeDtypeStruct((hh, tall, rows), f32),
            jax.ShapeDtypeStruct((8, rows), f32),
        ),
        in_specs=[pl.BlockSpec(memory_space=pltpu.SMEM)] + [vmem] * 6 + [hbm] * 2,
        out_specs=(vmem,) * 5,
        scratch_shapes=[
            pltpu.VMEM((3 * hh * PAD, width), bf16),
            pltpu.VMEM((hh * PAD, width), bf16),
            pltpu.VMEM((3 * hh * PAD, 1), f32),
            pltpu.VMEM((width, 3 * width), bf16),
            pltpu.VMEM((width, width), bf16),
            pltpu.VMEM((width, length), bf16),
            pltpu.VMEM((width, length), bf16),
            pltpu.VMEM((3, hh, PAD, length), bf16),
            pltpu.VMEM((3, hh, length, 128), bf16),
            pltpu.VMEM((hh, length, length), f32),
            pltpu.VMEM((hh, PAD, length), bf16),
            pltpu.VMEM((hh, PAD, length), bf16),
            pltpu.VMEM((hh, length, 128), bf16),
            pltpu.VMEM((2, hh, length, 128), f32),
            pltpu.VMEM((hh, 3, PAD, length), bf16),
            pltpu.VMEM((n, hh, PAD, tokens), bf16),
            pltpu.VMEM((hh, n, 3, PAD, tokens), bf16),
            pltpu.VMEM((3 * width, tokens), bf16),
            pltpu.VMEM((width, tokens), f32),
            pltpu.VMEM((ndp, across, rows), bf16),
            pltpu.VMEM((ndp, across, rows), bf16),
            pltpu.VMEM((hh, ndp, tall, rows), bf16),
            pltpu.VMEM((hh, ndp, tall, rows), bf16),
            pltpu.VMEM((ndp, 8, rows), f32),
            pltpu.VMEM((ndp, 8, rows), f32),
            pltpu.VMEM((8, rows), f32),
            pltpu.VMEM((n, 8, rows), f32),
            dma((2,)), dma((2, n)), dma((2, n)), dma((n,)), dma((n,)), dma((hh, n)), dma((hh, n)),
            dma((ndp,)), dma((ndp,)), dma((hh, ndp)), dma((hh, ndp)),
            dma((ndp,)), dma((ndp,)), dma((n,)), dma((n,)), dma((1 + hh,)),
        ],
        compiler_params=pltpu.CompilerParams(
            collective_id=0, has_side_effects=True, vmem_limit_bytes=63 * 1024 * 1024),
    )(
        survive, inputs[0], cotangent[0], ln_gain, ln_bias, qv_bias, proj_bias,
        w_qkv, w_proj,
    )
    grad_w_qkv = gqkv[:, :3 * hw].reshape(hh, 3, hw, rows).transpose(3, 1, 0, 2).reshape(rows, 3, hh * hw)
    grad_w_proj = gproj[:hh * hw]
    own = rows // n
    mine = lax.dynamic_slice_in_dim(small, me * own, own, 1)
    return (
        out[None], gin[None], grad_w_qkv, grad_w_proj,
        mine[0], mine[1], mine[2:4], mine[4],
    )


def solution(mesh):
    placed = (P("dp", "ctx", None), P("dp", "ctx", None), P("dp"), P(), P(), P(), P(), P(), P())
    return jax.shard_map(
        local,
        mesh=mesh,
        in_specs=placed,
        out_specs=(
            P("dp", "ctx", None),
            P("dp", "ctx", None),
            P("dp", None, "ctx"),
            P("ctx", "dp"),
            P(("dp", "ctx")),
            P(("dp", "ctx")),
            P(None, ("dp", "ctx")),
            P(("dp", "ctx")),
        ),
        check_vma=False,
    )
```
